32 devices in a mesh: col: 4 (over z), grp: 8 (over y, x, core).
Axes of the slice: x: 2, y: 2, z: 4, core: 2. Of those that a mesh axis runs over, the one named last changes fastest.
Arguments:
- factor_rows: float32 [1024, 8, 4, 512], P('grp', None, 'col'), may hold values from -3 to 3, as said below
- new_rows: float32 [4096, 8, 4, 512], P('grp', None, 'col'), may hold values from -0.5 to 0.5
Outputs:
- updated_rows: float32 [1024, 8, 4, 512], P('grp', None, 'col')
The draws below stay inside these ranges and needn't reach their ends.
Inputs may be any that keep to these rules, and one draw needn't show every extreme that they name: factor_rows is upper triangular in the global row and column numbers, with diagonal entries between 1 and 3.
All inputs are finite; a program needn't handle non-finite values.
Results may differ from the reference program's by a relative error of at most 0.00008.
Values sent between devices are 32-bit elements; how exact they have to be, the bound alone decides.
A program may use at most 128 MiB of HBM per device.

```python
import jax
import jax.numpy as jnp
from jax import lax

N = 16384
B = 512
ROWS_GRP = 512
NPAN = 8
M = 4096
N_COL = 4
N_GRP = 8


def draw_factor_rows(key, part):
    spread = N // (NPAN * B)
    shape = (2 * B, NPAN, spread, B)
    key_off, key_diag = jax.random.split(jax.random.fold_in(key, 11))
    row_index = jax.lax.broadcasted_iota(jnp.int32, shape, 0)
    column = (jax.lax.broadcasted_iota(jnp.int32, shape, 1) * spread + jax.lax.broadcasted_iota(jnp.int32, shape, 2)) * B + jax.lax.broadcasted_iota(jnp.int32, shape, 3)
    above = jax.random.normal(key_off, shape, jnp.float32)
    above = above * (2.0 * B) ** (-0.5)
    diagonal = jax.random.uniform(key_diag, shape, jnp.float32, 1.0, 3.0)
    return jnp.where(column > row_index, above, jnp.where(column == row_index, diagonal, 0.0)).astype(jnp.float32)


def levels(rng, extent, pieces, least, high):
    gain, own = 1.0, jax.random.fold_in(rng, 6)
    for axis_at, shards_of in pieces:
        heights = jnp.exp(jax.random.uniform(jax.random.fold_in(own, axis_at), (shards_of,), jnp.float32, least / len(pieces), high / len(pieces)))
        gain = gain * jnp.repeat(heights, extent[axis_at] // shards_of).reshape([-1 if axis == axis_at else 1 for axis in range(len(extent))])
    return gain


def noise(key, extent, scale, reach, shards=(), dtype=jnp.bfloat16):
    values = scale * jax.random.normal(key, extent, jnp.float32)
    if shards:
        values = values * levels(key, extent, shards, -0.22, 0.18)
    return jnp.clip(values, -reach, reach).astype(dtype)


def setup_inputs(seed: int = 0) -> dict:
    arg_keys = jax.random.split(jax.random.key(seed), 3)
    return {
        "factor_rows": draw_factor_rows(jax.random.fold_in(arg_keys[2], 71), 0),
        "new_rows": noise(arg_keys[1], (M, NPAN, N_COL, B), (2.0 / (ROWS_GRP * N_GRP) ** 0.5), 0.5, ((0, 8), (2, 4)), jnp.float32),
    }


def solve_lower(lower, right):
    return lax.linalg.triangular_solve(lower, right, left_side=True, lower=True)

def reference(factor_rows, new_rows):
    highest = lax.Precision.HIGHEST
    top = factor_rows.reshape(2 * B, N).astype(jnp.float32)
    data = new_rows.reshape(M, N).astype(jnp.float32)
    stacked = jnp.concatenate([top, data], 0)
    first = stacked[:, :B]
    second = stacked[:, B:2 * B]
    gram_one = jnp.dot(first.T, stacked, precision=highest)
    gram_two = jnp.dot(second.T, stacked, precision=highest)
    lower_one = jnp.linalg.cholesky(gram_one[:, :B])
    upper_one = solve_lower(lower_one, gram_one)
    cross = upper_one[:, B:2 * B]
    lower_two = jnp.linalg.cholesky(gram_two[:, B:2 * B] - jnp.dot(cross.T, cross, precision=highest))
    upper_two = solve_lower(lower_two, gram_two - jnp.dot(cross.T, upper_one, precision=highest))
    result = jnp.concatenate([upper_one, upper_two], 0)
    return result.reshape(2 * B, NPAN, N // (NPAN * B), B)
```

```python
import jax
import jax.numpy as jnp
from jax import lax
from jax.experimental import pallas as pl
from jax.experimental.pallas import tpu as pltpu
from jax.sharding import PartitionSpec as P

TILE = 128
SLAB = 8


def inverse_factor_tile(d):
    count = TILE // SLAB
    rows = [d[SLAB * q:SLAB * (q + 1), :] for q in range(count)]
    sub = lax.broadcasted_iota(jnp.int32, (SLAB, TILE), 0)
    lane = lax.broadcasted_iota(jnp.int32, (SLAB, TILE), 1)
    full = (SLAB, TILE)
    for q in range(count):
        at = SLAB * q
        inside = (lane >= at) & (lane < at + SLAB)
        slab = rows[q]
        cols = [jnp.broadcast_to(slab[:, at + j:at + j + 1], full) for j in range(SLAB)]
        t = jnp.where(inside, jnp.where(lane - at == sub, 1.0, 0.0), slab)
        pivots = jnp.ones(full, jnp.float32)
        for j in range(SLAB):
            p = jnp.broadcast_to(cols[j][j:j + 1, :], full)
            pivots = jnp.where(sub == j, p, pivots)
            if j == SLAB - 1:
                break
            m = jnp.where(sub > j, cols[j] * (1.0 / p), 0.0)
            for k in range(j + 1, SLAB):
                cols[k] = cols[k] - m * jnp.broadcast_to(cols[k][j:j + 1, :], full)
            t = t - m * jnp.broadcast_to(t[j:j + 1, :], full)
        y = lax.rsqrt(pivots)
        y = y * (1.5 - 0.5 * pivots * y * y)
        t = t * y
        rows[q] = t
        if q + 1 < count:
            turned = t.T
            lines = [jnp.broadcast_to(t[j:j + 1, :], full) for j in range(SLAB)]
            for i in range(q + 1, count):
                left = turned[SLAB * i:SLAB * (i + 1), :]
                total = jnp.where(inside, 0.0, rows[i])
                for j in range(SLAB):
                    total = total - jnp.broadcast_to(left[:, j:j + 1], full) * lines[j]
                rows[i] = total
    done = jnp.concatenate(rows, 0)
    r = lax.broadcasted_iota(jnp.int32, (TILE, TILE), 0)
    c = lax.broadcasted_iota(jnp.int32, (TILE, TILE), 1)
    return jnp.where(r >= c, done, 0.0)


def inverse_factor_kernel(s_ref, m_ref):
    n = s_ref.shape[0]
    count = n // TILE
    highest = lax.Precision.HIGHEST
    m_ref[...] = s_ref[...]
    r = lax.broadcasted_iota(jnp.int32, (TILE, TILE), 0)
    c = lax.broadcasted_iota(jnp.int32, (TILE, TILE), 1)
    eye = jnp.where(r == c, 1.0, 0.0).astype(jnp.float32)

    @pl.loop(0, count)
    def _(k):
        here = pl.ds(pl.multiple_of(k * TILE, TILE), TILE)
        inverse = inverse_factor_tile(m_ref[here, here])
        m_ref[here, here] = eye
        line = jnp.dot(inverse, m_ref[here, :], precision=highest, preferred_element_type=jnp.float32)
        m_ref[here, :] = line

        @pl.loop(k + 1, count)
        def _(i):
            there = pl.ds(pl.multiple_of(i * TILE, TILE), TILE)
            m_ref[there, here] = jnp.zeros((TILE, TILE), jnp.float32)
            m_ref[there, :] -= lax.dot_general(
                m_ref[here, there], m_ref[here, :], (((0,), (0,)), ((), ())),
                precision=highest, preferred_element_type=jnp.float32,
            )

    @pl.loop(0, count)
    def _(k):
        here = pl.ds(pl.multiple_of(k * TILE, TILE), TILE)
        row = lax.broadcasted_iota(jnp.int32, (TILE, n), 0) + k * TILE
        col = lax.broadcasted_iota(jnp.int32, (TILE, n), 1)
        m_ref[here, :] = jnp.where(row >= col, m_ref[here, :], 0.0)


def inverse_factor(s):
    n = s.shape[0]
    return pl.pallas_call(
        inverse_factor_kernel,
        out_shape=jax.ShapeDtypeStruct((n, n), jnp.float32),
        in_specs=[pl.BlockSpec(memory_space=pltpu.VMEM)],
        out_specs=pl.BlockSpec(memory_space=pltpu.VMEM),
        compiler_params=pltpu.CompilerParams(vmem_limit_bytes=24 * 2**20),
        cost_estimate=pl.CostEstimate(flops=60 * 10**9, bytes_accessed=8 * 2**20, transcendentals=0),
    )(s)


def leading_panels(panel, ncol):
    me = lax.axis_index("col")
    back = lax.ppermute(panel, "col", [(1, 0)])
    first = panel
    second = jnp.where(me == 0, back, panel)
    sent = panel
    for t in range(ncol - 1):
        pairs = [(t, t + 1)] + ([(t + 1, t + 2)] if t + 2 < ncol else [])
        sent = lax.ppermute(sent, "col", pairs)
        first = jnp.where(me == t + 1, sent, first)
        if t + 2 < ncol:
            second = jnp.where(me == t + 2, sent, second)
    return first, second


def make_shards(ncol, ngrp):
    def shards(factor_rows, new_rows):
        high, highest = lax.Precision.HIGH, lax.Precision.HIGHEST
        own_rows = factor_rows.shape[0]
        npanel = factor_rows.shape[1]
        width = factor_rows.shape[3]
        panels = [
            jnp.concatenate([factor_rows[:, p, 0, :], new_rows[:, p, 0, :]], 0)
            for p in range(npanel)
        ]
        total = panels[0].shape[0]
        cut = total // 2
        top = leading_panels(panels[0][:cut], ncol)
        low = leading_panels(panels[0][cut:], ncol)
        both = jnp.concatenate(
            [jnp.concatenate(top, 1), jnp.concatenate(low, 1)], 0
        )
        split = max(1, ngrp // npanel)
        piece = width // split
        turned = (((0,), (0,)), ((), ()))
        corner = lax.dot_general(both, both, turned, precision=highest, preferred_element_type=jnp.float32)
        corner = lax.psum(corner, "grp")
        parts = [
            lax.dot_general(
                both, x[:, q * piece:(q + 1) * piece], turned,
                precision=high, preferred_element_type=jnp.float32,
            )
            for x in panels for q in range(split)
        ]
        per = npanel * split // ngrp
        gram = jnp.stack(parts, 0)
        gram = lax.psum_scatter(gram, "grp", scatter_dimension=0, tiled=True)
        inverse = inverse_factor(corner)
        done = [
            jnp.dot(inverse, gram[p], precision=high, preferred_element_type=jnp.float32)
            for p in range(per)
        ]
        result = jnp.stack(done, 0).reshape(per, ngrp, own_rows, piece)
        result = lax.all_to_all(result, "grp", split_axis=1, concat_axis=0, tiled=True)
        result = result.reshape(npanel, split, own_rows, piece)
        return result.transpose(2, 0, 1, 3).reshape(own_rows, npanel, 1, width)

    return shards


def solution(mesh):
    placed = P("grp", None, "col", None)
    return jax.shard_map(
        make_shards(mesh.shape["col"], mesh.shape["grp"]),
        mesh=mesh, in_specs=(placed, placed), out_specs=placed, check_vma=False,
    )
```

```python
import functools

import jax
import jax.numpy as jnp
from jax import lax
from jax.experimental import pallas as pl
from jax.experimental.pallas import tpu as pltpu
from jax.sharding import PartitionSpec as P

TILE = 128
SLAB = 8


def inverse_factor_tile(d):
    count = TILE // SLAB
    rows = [d[SLAB * q:SLAB * (q + 1), :] for q in range(count)]
    sub = lax.broadcasted_iota(jnp.int32, (SLAB, TILE), 0)
    lane = lax.broadcasted_iota(jnp.int32, (SLAB, TILE), 1)
    full = (SLAB, TILE)
    for q in range(count):
        at = SLAB * q
        inside = (lane >= at) & (lane < at + SLAB)
        slab = rows[q]
        cols = [jnp.broadcast_to(slab[:, at + j:at + j + 1], full) for j in range(SLAB)]
        t = jnp.where(inside, jnp.where(lane - at == sub, 1.0, 0.0), slab)
        pivots = jnp.ones(full, jnp.float32)
        for j in range(SLAB):
            p = jnp.broadcast_to(cols[j][j:j + 1, :], full)
            pivots = jnp.where(sub == j, p, pivots)
            if j == SLAB - 1:
                break
            m = jnp.where(sub > j, cols[j] * (1.0 / p), 0.0)
            for k in range(j + 1, SLAB):
                cols[k] = cols[k] - m * jnp.broadcast_to(cols[k][j:j + 1, :], full)
            t = t - m * jnp.broadcast_to(t[j:j + 1, :], full)
        y = lax.rsqrt(pivots)
        y = y * (1.5 - 0.5 * pivots * y * y)
        t = t * y
        rows[q] = t
        if q + 1 < count:
            turned = t.T
            lines = [jnp.broadcast_to(t[j:j + 1, :], full) for j in range(SLAB)]
            for i in range(q + 1, count):
                left = turned[SLAB * i:SLAB * (i + 1), :]
                total = jnp.where(inside, 0.0, rows[i])
                for j in range(SLAB):
                    total = total - jnp.broadcast_to(left[:, j:j + 1], full) * lines[j]
                rows[i] = total
    done = jnp.concatenate(rows, 0)
    r = lax.broadcasted_iota(jnp.int32, (TILE, TILE), 0)
    c = lax.broadcasted_iota(jnp.int32, (TILE, TILE), 1)
    return jnp.where(r >= c, done, 0.0)


def upper_tiles(n):
    count = n // TILE
    return [(i, j) for i in range(count) for j in range(i, count)]


def corner_sum_kernel(n, s_ref, out_ref, packed, slots, send_a, recv_a, send_b, recv_b):
    me = lax.axis_index("grp")
    rows = packed.shape[0] // n
    mesh_id = pl.DeviceIdType.MESH
    peers = [lax.rem(me + step, n) for step in range(1, n)]
    barrier = pltpu.get_barrier_semaphore()
    for peer in peers:
        pl.semaphore_signal(barrier, inc=1, device_id={"grp": peer}, device_id_type=mesh_id)
    for at, (i, j) in enumerate(upper_tiles(s_ref.shape[0])):
        packed[at * TILE:(at + 1) * TILE, :] = s_ref[i * TILE:(i + 1) * TILE, j * TILE:(j + 1) * TILE]
    pl.semaphore_wait(barrier, n - 1)
    mine = pl.ds(pl.multiple_of(me * rows, 8), rows)
    scatter = []
    for at, peer in enumerate(peers):
        copy = pltpu.make_async_remote_copy(
            src_ref=packed.at[pl.ds(pl.multiple_of(peer * rows, 8), rows)],
            dst_ref=slots.at[at],
            send_sem=send_a.at[at], recv_sem=recv_a.at[at],
            device_id={"grp": peer}, device_id_type=mesh_id,
        )
        copy.start()
        scatter.append(copy)
    total = packed[mine, :]
    for at in range(n - 1):
        scatter[at].wait_recv()
        total = total + slots[at]
    out_ref[mine, :] = total
    gather = []
    for at, peer in enumerate(peers):
        copy = pltpu.make_async_remote_copy(
            src_ref=out_ref.at[mine], dst_ref=out_ref.at[mine],
            send_sem=send_b.at[at], recv_sem=recv_b.at[at],
            device_id={"grp": peer}, device_id_type=mesh_id,
        )
        copy.start()
        gather.append(copy)
    for at, peer in enumerate(peers):
        back = lax.rem(me + n - 1 - at, n)
        pltpu.make_async_remote_copy(
            src_ref=out_ref.at[mine],
            dst_ref=out_ref.at[pl.ds(pl.multiple_of(back * rows, 8), rows)],
            send_sem=send_b.at[at], recv_sem=recv_b.at[at],
            device_id={"grp": peer}, device_id_type=mesh_id,
        ).wait_recv()
        scatter[at].wait_send()
        gather[at].wait_send()


def corner_sum(s, ngrp):
    total = len(upper_tiles(s.shape[0])) * TILE
    dma = pltpu.SemaphoreType.DMA((ngrp - 1,))
    return pl.pallas_call(
        functools.partial(corner_sum_kernel, ngrp),
        out_shape=jax.ShapeDtypeStruct((total, TILE), jnp.float32),
        in_specs=[pl.BlockSpec(memory_space=pltpu.VMEM)],
        out_specs=pl.BlockSpec(memory_space=pltpu.VMEM),
        scratch_shapes=[
            pltpu.VMEM((total, TILE), jnp.float32),
            pltpu.VMEM((ngrp - 1, total // ngrp, TILE), jnp.float32),
            dma, dma, dma, dma,
        ],
        compiler_params=pltpu.CompilerParams(
            collective_id=0, has_side_effects=True, vmem_limit_bytes=24 * 2**20
        ),
        cost_estimate=pl.CostEstimate(flops=40 * 10**9, bytes_accessed=8 * 2**20, transcendentals=0),
    )(s)


def inverse_factor_kernel(s_ref, m_ref):
    n = m_ref.shape[0]
    count = n // TILE
    highest = lax.Precision.HIGHEST
    for at, (i, j) in enumerate(upper_tiles(n)):
        m_ref[i * TILE:(i + 1) * TILE, j * TILE:(j + 1) * TILE] = s_ref[at * TILE:(at + 1) * TILE, :]
    r = lax.broadcasted_iota(jnp.int32, (TILE, TILE), 0)
    c = lax.broadcasted_iota(jnp.int32, (TILE, TILE), 1)
    eye = jnp.where(r == c, 1.0, 0.0).astype(jnp.float32)

    @pl.loop(0, count)
    def _(k):
        here = pl.ds(pl.multiple_of(k * TILE, TILE), TILE)
        inverse = inverse_factor_tile(m_ref[here, here])
        m_ref[here, here] = eye
        line = jnp.dot(inverse, m_ref[here, :], precision=highest, preferred_element_type=jnp.float32)
        m_ref[here, :] = line

        @pl.loop(k + 1, count)
        def _(i):
            there = pl.ds(pl.multiple_of(i * TILE, TILE), TILE)
            m_ref[there, here] = jnp.zeros((TILE, TILE), jnp.float32)
            m_ref[there, :] -= lax.dot_general(
                m_ref[here, there], m_ref[here, :], (((0,), (0,)), ((), ())),
                precision=highest, preferred_element_type=jnp.float32,
            )

    @pl.loop(0, count)
    def _(k):
        here = pl.ds(pl.multiple_of(k * TILE, TILE), TILE)
        row = lax.broadcasted_iota(jnp.int32, (TILE, n), 0) + k * TILE
        col = lax.broadcasted_iota(jnp.int32, (TILE, n), 1)
        m_ref[here, :] = jnp.where(row >= col, m_ref[here, :], 0.0)


def inverse_factor(s, n):
    return pl.pallas_call(
        inverse_factor_kernel,
        out_shape=jax.ShapeDtypeStruct((n, n), jnp.float32),
        in_specs=[pl.BlockSpec(memory_space=pltpu.VMEM)],
        out_specs=pl.BlockSpec(memory_space=pltpu.VMEM),
        compiler_params=pltpu.CompilerParams(vmem_limit_bytes=24 * 2**20),
        cost_estimate=pl.CostEstimate(flops=60 * 10**9, bytes_accessed=8 * 2**20, transcendentals=0),
    )(s)


def chain(panel, ncol):
    back = lax.ppermute(panel, "col", [(1, 0)])
    sent, steps = panel, []
    for t in range(ncol - 1):
        pairs = [(t, t + 1)] + ([(t + 1, t + 2)] if t + 2 < ncol else [])
        sent = lax.ppermute(sent, "col", pairs)
        steps.append(sent)
    return back, steps


def chosen(panel, back, steps):
    me = lax.axis_index("col")
    first, second = panel, jnp.where(me == 0, back, panel)
    for t, sent in enumerate(steps):
        first = jnp.where(me == t + 1, sent, first)
        if t + 1 < len(steps):
            second = jnp.where(me == t + 2, sent, second)
    return first, second


def make_shards(ncol, ngrp):
    def shards(factor_rows, new_rows):
        high, highest = lax.Precision.HIGH, lax.Precision.HIGHEST
        own_rows = factor_rows.shape[0]
        npanel = factor_rows.shape[1]
        width = factor_rows.shape[3]
        lead = jnp.concatenate([factor_rows[:, 0, 0, :], new_rows[:, 0, 0, :]], 0)
        half = width // 2
        lead, factor_rows, new_rows = lax.optimization_barrier((lead, factor_rows, new_rows))
        panels = [lead] + [
            jnp.concatenate([factor_rows[:, p, 0, :], new_rows[:, p, 0, :]], 0)
            for p in range(1, npanel)
        ]
        split = max(1, ngrp // npanel)
        piece = width // split
        per = npanel * split // ngrp
        turned = (((0,), (0,)), ((), ()))
        back_a, steps_a = chain(lead[:, :half], ncol)
        back_b, steps_b = chain(lead[:, half:], ncol)
        back_a, steps_a, back_b, early_b = lax.optimization_barrier(
            (back_a, steps_a, back_b, steps_b[:-1])
        )
        first_a, second_a = chosen(lead[:, :half], back_a, steps_a)
        first_b, second_b = chosen(lead[:, half:], back_b, early_b + steps_b[-1:])

        def gram_rows(left):
            return jnp.stack([
                lax.dot_general(
                    left, x[:, q * piece:(q + 1) * piece], turned,
                    precision=high, preferred_element_type=jnp.float32,
                )
                for x in panels for q in range(split)
            ], 0)

        gram_a = gram_rows(jnp.concatenate([first_a, second_a], 1))
        sum_a = lax.psum_scatter(gram_a, "grp", scatter_dimension=0, tiled=True)
        both = jnp.concatenate([first_a, first_b, second_a, second_b], 1)
        corner = lax.dot_general(both, both, turned, precision=highest, preferred_element_type=jnp.float32)
        gram_b = gram_rows(jnp.concatenate([first_b, second_b], 1))
        gram_b, corner = lax.optimization_barrier((gram_b, corner))
        sum_b = lax.psum_scatter(gram_b, "grp", scatter_dimension=0, tiled=True)
        inverse = inverse_factor(corner_sum(corner, ngrp), 2 * width)
        gram = jnp.concatenate(
            [sum_a[:, :half], sum_b[:, :half], sum_a[:, half:], sum_b[:, half:]], 1
        )
        done = [
            jnp.dot(inverse, gram[p], precision=high, preferred_element_type=jnp.float32)
            for p in range(per)
        ]
        result = jnp.stack(done, 0).reshape(per, ngrp, own_rows, piece)
        result = lax.all_to_all(result, "grp", split_axis=1, concat_axis=0, tiled=True)
        result = result.reshape(npanel, split, own_rows, piece)
        return result.transpose(2, 0, 1, 3).reshape(own_rows, npanel, 1, width)

    return shards


def solution(mesh):
    placed = P("grp", None, "col", None)
    return jax.shard_map(
        make_shards(mesh.shape["col"], mesh.shape["grp"]),
        mesh=mesh, in_specs=(placed, placed), out_specs=placed, check_vma=False,
    )
```

```python
import jax
import jax.numpy as jnp
from jax import lax
from jax.experimental import pallas as pl
from jax.experimental.pallas import tpu as pltpu
from jax.sharding import PartitionSpec as P

TILE = 128
SLAB = 8


def inverse_factor_tile(d):
    count = TILE // SLAB
    rows = [d[SLAB * q:SLAB * (q + 1), :] for q in range(count)]
    sub = lax.broadcasted_iota(jnp.int32, (SLAB, TILE), 0)
    lane = lax.broadcasted_iota(jnp.int32, (SLAB, TILE), 1)
    full = (SLAB, TILE)
    for q in range(count):
        at = SLAB * q
        inside = (lane >= at) & (lane < at + SLAB)
        slab = rows[q]
        cols = [jnp.broadcast_to(slab[:, at + j:at + j + 1], full) for j in range(SLAB)]
        t = jnp.where(inside, jnp.where(lane - at == sub, 1.0, 0.0), slab)
        pivots = jnp.ones(full, jnp.float32)
        for j in range(SLAB):
            p = jnp.broadcast_to(cols[j][j:j + 1, :], full)
            pivots = jnp.where(sub == j, p, pivots)
            if j == SLAB - 1:
                break
            m = jnp.where(sub > j, cols[j] * (1.0 / p), 0.0)
            for k in range(j + 1, SLAB):
                cols[k] = cols[k] - m * jnp.broadcast_to(cols[k][j:j + 1, :], full)
            t = t - m * jnp.broadcast_to(t[j:j + 1, :], full)
        y = lax.rsqrt(pivots)
        y = y * (1.5 - 0.5 * pivots * y * y)
        t = t * y
        rows[q] = t
        if q + 1 < count:
            turned = t.T
            lines = [jnp.broadcast_to(t[j:j + 1, :], full) for j in range(SLAB)]
            for i in range(q + 1, count):
                left = turned[SLAB * i:SLAB * (i + 1), :]
                total = jnp.where(inside, 0.0, rows[i])
                for j in range(SLAB):
                    total = total - jnp.broadcast_to(left[:, j:j + 1], full) * lines[j]
                rows[i] = total
    done = jnp.concatenate(rows, 0)
    r = lax.broadcasted_iota(jnp.int32, (TILE, TILE), 0)
    c = lax.broadcasted_iota(jnp.int32, (TILE, TILE), 1)
    return jnp.where(r >= c, done, 0.0)


def inverse_factor_kernel(s_ref, m_ref):
    n = m_ref.shape[0]
    count = n // TILE
    highest = lax.Precision.HIGHEST
    band, at = s_ref.shape[0], 0
    for top in range(0, n, band):
        m_ref[top:top + band, top:] = s_ref[:, at:at + n - top]
        at += n - top
    r = lax.broadcasted_iota(jnp.int32, (TILE, TILE), 0)
    c = lax.broadcasted_iota(jnp.int32, (TILE, TILE), 1)
    eye = jnp.where(r == c, 1.0, 0.0).astype(jnp.float32)

    @pl.loop(0, count)
    def _(k):
        here = pl.ds(pl.multiple_of(k * TILE, TILE), TILE)
        inverse = inverse_factor_tile(m_ref[here, here])
        m_ref[here, here] = eye
        line = jnp.dot(inverse, m_ref[here, :], precision=highest, preferred_element_type=jnp.float32)
        m_ref[here, :] = line

        @pl.loop(k + 1, count)
        def _(i):
            there = pl.ds(pl.multiple_of(i * TILE, TILE), TILE)
            m_ref[there, here] = jnp.zeros((TILE, TILE), jnp.float32)
            m_ref[there, :] -= lax.dot_general(
                m_ref[here, there], m_ref[here, :], (((0,), (0,)), ((), ())),
                precision=highest, preferred_element_type=jnp.float32,
            )

    @pl.loop(0, count)
    def _(k):
        here = pl.ds(pl.multiple_of(k * TILE, TILE), TILE)
        row = lax.broadcasted_iota(jnp.int32, (TILE, n), 0) + k * TILE
        col = lax.broadcasted_iota(jnp.int32, (TILE, n), 1)
        m_ref[here, :] = jnp.where(row >= col, m_ref[here, :], 0.0)


def inverse_factor(s, n):
    return pl.pallas_call(
        inverse_factor_kernel,
        out_shape=jax.ShapeDtypeStruct((n, n), jnp.float32),
        in_specs=[pl.BlockSpec(memory_space=pltpu.VMEM)],
        out_specs=pl.BlockSpec(memory_space=pltpu.VMEM),
        compiler_params=pltpu.CompilerParams(vmem_limit_bytes=24 * 2**20),
        cost_estimate=pl.CostEstimate(flops=60 * 10**9, bytes_accessed=8 * 2**20, transcendentals=0),
    )(s)


def chain(panel, ncol):
    back = lax.ppermute(panel, "col", [(1, 0)])
    sent, steps = panel, []
    for t in range(ncol - 1):
        pairs = [(t, t + 1)] + ([(t + 1, t + 2)] if t + 2 < ncol else [])
        sent = lax.ppermute(sent, "col", pairs)
        steps.append(sent)
    return back, steps


def chosen(panel, back, steps):
    me = lax.axis_index("col")
    first, second = panel, jnp.where(me == 0, back, panel)
    for t, sent in enumerate(steps):
        first = jnp.where(me == t + 1, sent, first)
        if t + 1 < len(steps):
            second = jnp.where(me == t + 2, sent, second)
    return first, second


def make_shards(ncol, ngrp):
    def shards(factor_rows, new_rows):
        high, highest = lax.Precision.HIGH, lax.Precision.HIGHEST
        own_rows = factor_rows.shape[0]
        npanel = factor_rows.shape[1]
        width = factor_rows.shape[3]
        lead = jnp.concatenate([factor_rows[:, 0, 0, :], new_rows[:, 0, 0, :]], 0)
        half = width // 2
        lead, factor_rows, new_rows = lax.optimization_barrier((lead, factor_rows, new_rows))
        panels = [lead] + [
            jnp.concatenate([factor_rows[:, p, 0, :], new_rows[:, p, 0, :]], 0)
            for p in range(1, npanel)
        ]
        split = max(1, ngrp // npanel)
        piece = width // split
        per = npanel * split // ngrp
        turned = (((0,), (0,)), ((), ()))
        back_a, steps_a = chain(lead[:, :half], ncol)
        back_b, steps_b = chain(lead[:, half:], ncol)
        back_a, steps_a, back_b, steps_b = lax.optimization_barrier(
            (back_a, steps_a, back_b, steps_b)
        )
        first_a, second_a = chosen(lead[:, :half], back_a, steps_a)
        first_b, second_b = chosen(lead[:, half:], back_b, steps_b)

        def gram_rows(left):
            return jnp.stack([
                lax.dot_general(
                    left, x[:, q * piece:(q + 1) * piece], turned,
                    precision=high, preferred_element_type=jnp.float32,
                )
                for x in panels for q in range(split)
            ], 0)

        both = jnp.concatenate([first_a, first_b, second_a, second_b], 1)
        packed = jnp.concatenate([
            lax.dot_general(
                both[:, at:at + half], both[:, at:], turned,
                precision=highest, preferred_element_type=jnp.float32,
            )
            for at in range(0, 2 * width, half)
        ], 1)
        packed, both = lax.optimization_barrier((packed, both))
        packed = lax.psum(packed, "grp")
        gram = lax.psum_scatter(gram_rows(both), "grp", scatter_dimension=0, tiled=True)
        inverse = inverse_factor(packed, 2 * width)
        done = [
            jnp.dot(inverse, gram[p], precision=high, preferred_element_type=jnp.float32)
            for p in range(per)
        ]
        result = jnp.stack(done, 0).reshape(per, ngrp, own_rows, piece)
        result = lax.all_to_all(result, "grp", split_axis=1, concat_axis=0, tiled=True)
        result = result.reshape(npanel, split, own_rows, piece)
        return result.transpose(2, 0, 1, 3).reshape(own_rows, npanel, 1, width)

    return shards


def solution(mesh):
    placed = P("grp", None, "col", None)
    return jax.shard_map(
        make_shards(mesh.shape["col"], mesh.shape["grp"]),
        mesh=mesh, in_specs=(placed, placed), out_specs=placed, check_vma=False,
    )
```
